32 devices in a mesh: leaf: 4 (over y, x), blk: 8 (over z, core).
Axes of the slice: x: 2, y: 2, z: 4, core: 2. Of those that a mesh axis runs over, the one named last changes fastest.
Arguments:
- diag_blocks: float32 [4, 512, 512], P('leaf'), as said below
- panel: float32 [4, 32, 256, 512], P('leaf', 'blk'), may hold values from -1.2 to 1.2
- local_targets: bfloat16 [4, 640, 256, 256], P('leaf', 'blk'), may hold values from -6 to 6
- local_pairs: int32 [4, 640, 2], P('leaf', 'blk'), may hold values from -1 to 31, as said below
- top_targets: bfloat16 [8, 16, 256, 256], P('blk', 'leaf'), may hold values from -6 to 6
- top_pairs: int32 [8, 16, 2], P('blk'), may hold values from 0 to 63
- top_pattern: int32 [4, 64], P('leaf'), may hold values from -1 to 31, as said below
Outputs:
- panel_factor: bfloat16 [4, 32, 256, 512], P('leaf', 'blk')
- local_updated: bfloat16 [4, 640, 256, 256], P('leaf', 'blk')
- top_updated: bfloat16 [8, 16, 256, 256], P('blk', 'leaf')
The draws below stay inside these ranges and needn't reach their ends.
Inputs may be any that keep to these rules, and one draw needn't show every extreme that they name: Each diag_blocks[g] is symmetric positive definite with smallest eigenvalue 0.5 or more. `local_pairs`: empty slots hold -1 in both columns; on each device the live slots come first; some device has all 80 slots live. `top_pattern`: in each group every panel row 0 to 31 stands at exactly one ancestor row; the other ancestor rows hold -1.
All inputs are finite; a program needn't handle non-finite values.
Results may differ from the reference program's by a relative error of at most 0.014.
Values may be sent and summed in bfloat16 or wider, within the bound.
A program may use at most 192 MiB of HBM per device.

```python
import jax
import jax.numpy as jnp
from jax import lax

B = 256
TOP_DEV = 4
TL_DEV = 80
RG = 32
NA = 64
N_LEAF = 4
N_BLK = 8


def draw_diag_blocks(key, part):
    order_size = 2 * B
    base = jax.random.normal(key, (N_LEAF, order_size, order_size), jnp.float32)
    gram = jnp.einsum('gik,gjk->gij', base, base, precision=lax.Precision.HIGHEST) / order_size
    return gram + 0.5 * jnp.eye(order_size, dtype=jnp.float32)[None]


def draw_local_pairs(key, part):
    total = N_LEAF * N_BLK
    key_draws, key_full, key_rows = jax.random.split(key, 3)
    draws = jax.random.randint(key_draws, (total,), 1, TL_DEV + 1)
    counts = jnp.maximum(draws * draws // TL_DEV, 1)
    fullest = jax.random.randint(key_full, (), 0, total)
    counts = jnp.where(jnp.arange(total) == fullest, TL_DEV, counts)
    chosen = jax.random.randint(key_rows, (total, TL_DEV, 2), 0, RG)
    live = jnp.arange(TL_DEV)[None, :] < counts[:, None]
    pairs = jnp.where(live[:, :, None], chosen, -1)
    return pairs.reshape(N_LEAF, N_BLK * TL_DEV, 2).astype(jnp.int32)


def draw_top_pattern(key, part):
    group_keys = jax.random.split(key, N_LEAF)

    def one_group(group_key):
        ordering = jax.random.permutation(group_key, NA)
        ranking = jnp.argsort(ordering)
        return jnp.where(ranking < RG, ranking, -1)
    return jax.vmap(one_group)(group_keys).astype(jnp.int32)


def with_ends(result, key, least, top_value):
    longest = result.shape.index(max(result.shape))
    spots = []
    for shift in (0, 1):
        where = [jax.random.randint(jax.random.fold_in(key, axis), (), 0, length) for axis, length in enumerate(result.shape)]
        where[longest] = (where[longest] + shift) % result.shape[longest]
        spots.append(tuple(where))
    return result.at[spots[0]].set(least).at[spots[1]].set(top_value)


def levels(stream_key, extent, shards, least, top_value):
    gain, own = 1.0, jax.random.fold_in(stream_key, 6)
    for position, parts in shards:
        steps = jnp.exp(jax.random.uniform(jax.random.fold_in(own, position), (parts,), jnp.float32, least / len(shards), top_value / len(shards)))
        gain = gain * jnp.repeat(steps, extent[position] // parts).reshape([-1 if axis == position else 1 for axis in range(len(extent))])
    return gain


def scatter_about(own_key, extent, deviation, reach, cuts=(), kind=jnp.bfloat16):
    entries = jax.random.normal(own_key, extent, jnp.float32) * deviation
    if len(cuts) > 0:
        entries = levels(own_key, extent, cuts, -0.22, 0.18) * entries
    return jnp.clip(entries, min=-reach, max=reach).astype(kind)


def setup_inputs(seed: int = 0) -> dict:
    splits = jax.random.split(jax.random.key(seed), 8)
    diag_blocks = draw_diag_blocks(jax.random.fold_in(splits[7], 71), 0)
    panel = scatter_about(splits[1], (N_LEAF, RG, B, 2 * B), 0.2, 1.2, ((0, 4), (1, 8)), jnp.float32)
    local_targets = scatter_about(splits[2], (N_LEAF, N_BLK * TL_DEV, B, B), 1.0, 6.0, ((0, 4), (1, 8)))
    local_pairs = draw_local_pairs(jax.random.fold_in(splits[7], 71), 0)
    top_targets = scatter_about(splits[4], (N_BLK, N_LEAF * TOP_DEV, B, B), 1.0, 6.0, ((0, 8), (1, 4)))
    top_pairs = with_ends(jax.random.randint(splits[5], (N_BLK, N_LEAF * TOP_DEV, 2), 0, NA), jax.random.fold_in(splits[5], 1), 0, NA - 1).astype(jnp.int32)
    top_pattern = draw_top_pattern(jax.random.fold_in(splits[7], 71), 0)
    return dict(diag_blocks=diag_blocks, panel=panel, local_targets=local_targets, local_pairs=local_pairs, top_targets=top_targets, top_pairs=top_pairs, top_pattern=top_pattern)


def factor_group(diagonal, rows):
    width = diagonal.shape[0] // 2
    count = rows.shape[0]
    factor_full = jnp.linalg.cholesky(diagonal)
    upper_left = factor_full[:width, :width]
    lower_left = factor_full[width:, :width]
    lower_right = factor_full[width:, width:]
    flat = rows.reshape(count * width, 2 * width)
    first = jax.scipy.linalg.solve_triangular(upper_left, flat[:, :width].T, lower=True).T
    reduced = flat[:, width:] - jnp.dot(first, lower_left.T, precision=lax.Precision.HIGHEST)
    second = jax.scipy.linalg.solve_triangular(lower_right, reduced.T, lower=True).T
    joined = jnp.concatenate([first, second], axis=1)
    return joined.reshape(count, width, 2 * width).astype(jnp.bfloat16)

def pair_product(rows_float, left_index, right_index):
    left_rows = jnp.take(rows_float, left_index, axis=0)
    right_rows = jnp.take(rows_float, right_index, axis=0)
    return jnp.einsum('tik,tjk->tij', left_rows, right_rows, precision=lax.Precision.HIGHEST)

def reference(diag_blocks, panel, local_targets, local_pairs, top_targets, top_pairs, top_pattern):
    groups = diag_blocks.shape[0]
    factors = [factor_group(diag_blocks[g], panel[g]) for g in range(groups)]
    panel_factor = jnp.stack(factors, axis=0)
    rows_all = panel_factor.astype(jnp.float32)
    width = panel.shape[2]
    local_list = []
    for g in range(groups):
        rows_float = rows_all[g]

        def slot_block(items):
            target_block, pair_block = items
            live = pair_block[:, 0] >= 0
            product = pair_product(rows_float, jnp.maximum(pair_block[:, 0], 0), jnp.maximum(pair_block[:, 1], 0))
            fresh = target_block.astype(jnp.float32) - jnp.where(live[:, None, None], product, jnp.float32(0.0))
            return fresh.astype(jnp.bfloat16)
        slots = local_targets.shape[1]
        blocked = lax.map(slot_block, (local_targets[g].reshape(slots // 8, 8, width, width), local_pairs[g].reshape(slots // 8, 8, 2)))
        local_list.append(blocked.reshape(slots, width, width))
    local_updated = jnp.stack(local_list, axis=0)

    def column(items):
        target_column, pair_column = items
        total = jnp.zeros(target_column.shape, jnp.float32)
        for g in range(groups):
            left_pos = jnp.take(top_pattern[g], pair_column[:, 0])
            right_pos = jnp.take(top_pattern[g], pair_column[:, 1])
            present = (left_pos >= 0) & (right_pos >= 0)
            product = pair_product(rows_all[g], jnp.maximum(left_pos, 0), jnp.maximum(right_pos, 0))
            total = total + jnp.where(present[:, None, None], product, jnp.float32(0.0))
        return (target_column.astype(jnp.float32) - total).astype(jnp.bfloat16)
    top_updated = lax.map(column, (top_targets, top_pairs))
    return (panel_factor, local_updated, top_updated)
```

```python
import functools

import jax
import jax.numpy as jnp
from jax import lax
from jax.experimental import pallas as pl
from jax.experimental.pallas import tpu as pltpu
from jax.sharding import PartitionSpec as P

NB = 128
HI = lax.Precision.HIGHEST
VMEM_LIMIT = 56 * 1024 * 1024


def mm(a, b, contract, precision=HI):
    return lax.dot_general(
        a, b, ((contract[:1], contract[1:]), ((), ())),
        precision=precision, preferred_element_type=jnp.float32,
    )


def eliminate(block, inv_ref):
    groups = NB // 8
    d = [block[8 * g:8 * g + 8, :] for g in range(groups)]
    row = lax.broadcasted_iota(jnp.int32, (8, NB), 0)
    col = lax.broadcasted_iota(jnp.int32, (8, NB), 1)
    e = [jnp.where(row + 8 * g == col, 1.0, 0.0).astype(jnp.float32) for g in range(groups)]
    for j in range(NB):
        g, r = divmod(j, 8)
        drow = d[g][r:r + 1, :]
        erow = e[g][r:r + 1, :]
        pivot = jnp.broadcast_to(drow[:, j:j + 1], (1, NB))
        inv_ref[j:j + 1, :] = erow * lax.rsqrt(pivot)
        inverse = 1.0 / pivot
        dscaled = drow * inverse
        escaled = erow * inverse
        for h in range(g if r < 7 else g + 1, groups):
            factor = jnp.broadcast_to(d[h][:, j:j + 1], (8, NB))
            d[h] = d[h] - factor * dscaled
            e[h] = e[h] - factor * escaled


def factor_step(last, s_ref, a_ref, x_ref, *rest):
    inv_ref = rest[-1]
    eliminate(s_ref[0:NB, 0:NB], inv_ref)
    inverse = inv_ref[...]
    x = mm(a_ref[:, 0:NB], inverse, (1, 1))
    x_ref[...] = x.astype(x_ref.dtype)
    if not last:
        s_next, a_next = rest[:2]
        upper = mm(inverse, s_ref[0:NB, NB:], (1, 0))
        s_next[...] = s_ref[NB:, NB:] - mm(upper, upper, (0, 0))
        a_next[...] = a_ref[:, NB:] - mm(x, upper, (1, 0))


def run_factor_step(s, a):
    order, rows = s.shape[0], a.shape[0]
    last = order == NB
    out = [jax.ShapeDtypeStruct((rows, NB), jnp.bfloat16)]
    if not last:
        out += [
            jax.ShapeDtypeStruct((order - NB, order - NB), jnp.float32),
            jax.ShapeDtypeStruct((rows, order - NB), jnp.float32),
        ]
    vmem = pl.BlockSpec(memory_space=pltpu.VMEM)
    return pl.pallas_call(
        functools.partial(factor_step, last),
        out_shape=out,
        in_specs=[vmem, vmem],
        out_specs=[vmem] * len(out),
        scratch_shapes=[pltpu.VMEM((NB, NB), jnp.float32)],
        compiler_params=pltpu.CompilerParams(vmem_limit_bytes=VMEM_LIMIT),
        cost_estimate=pl.CostEstimate(flops=20_000_000_000, bytes_accessed=8_000_000, transcendentals=0),
        name="factor_step",
    )(s, a)


def product(refs, p, q):
    left = jnp.concatenate([ref[p] for ref in refs], axis=1)
    right = jnp.concatenate([ref[q] for ref in refs], axis=1)
    return mm(left, right, (1, 1), None)


def top_kernel(per_step, pairs, *refs):
    slices, out = refs[:-1], refs[-1]
    base = pl.program_id(0) * per_step
    for s in range(per_step):
        p, q = pairs[0, base + s], pairs[1, base + s]
        present = (p >= 0) & (q >= 0)

        @pl.when(present)
        def _():
            out[s] = product(slices, p, q).astype(out.dtype)

        @pl.when(jnp.logical_not(present))
        def _():
            out[s] = jnp.zeros(out.shape[1:], out.dtype)


def local_kernel(per_step, pairs, *refs):
    slices, target, out = refs[:-2], refs[-2], refs[-1]
    base = pl.program_id(0) * per_step
    for s in range(per_step):
        p, q = pairs[0, base + s], pairs[1, base + s]

        @pl.when(p >= 0)
        def _():
            fresh = target[s].astype(jnp.float32) - product(slices, p, q)
            out[s] = fresh.astype(out.dtype)

        @pl.when(p < 0)
        def _():
            out[s] = target[s]


def run_pairs(kernel, pairs, slices, targets, count, per_step, name):
    rows, width, depth = slices[0].shape
    whole = pl.BlockSpec((rows, width, depth), lambda i, pairs: (0, 0, 0), pipeline_mode=pl.Buffered(1))
    block = pl.BlockSpec((per_step, width, width), lambda i, pairs: (i, 0, 0))
    extra = [] if targets is None else [targets]
    return pl.pallas_call(
        functools.partial(kernel, per_step),
        grid_spec=pltpu.PrefetchScalarGridSpec(
            num_scalar_prefetch=1,
            grid=(count // per_step,),
            in_specs=[whole] * len(slices) + [block] * len(extra),
            out_specs=block,
        ),
        out_shape=jax.ShapeDtypeStruct((count, width, width), jnp.bfloat16),
        compiler_params=pltpu.CompilerParams(vmem_limit_bytes=VMEM_LIMIT),
        cost_estimate=pl.CostEstimate(
            flops=2 * count * width * width * depth * len(slices),
            bytes_accessed=4 * count * width * width,
            transcendentals=0,
        ),
        name=name,
    )(pairs, *slices, *extra)


def on_device(diag_blocks, panel, local_targets, local_pairs, top_targets, top_pairs, top_pattern):
    s = diag_blocks[0]
    count, width, columns = panel.shape[1:]
    a = panel[0].reshape(count * width, columns)
    pattern = top_pattern[0]
    ancestors = jnp.arange(pattern.shape[0], dtype=jnp.int32)

    def lookup(ids):
        return jnp.sum(jnp.where(ids[:, None] == ancestors[None, :], pattern[None, :], 0), axis=1)

    positions = jnp.stack([lookup(top_pairs[0, :, 0]), lookup(top_pairs[0, :, 1])])
    pairs = local_pairs[0].T

    own, slices = [], []
    while True:
        x, *state = run_factor_step(s, a)
        x = x.reshape(count, width, NB)
        own.append(x)
        slices.append(lax.all_gather(x, "blk", axis=0, tiled=True))
        if not state:
            break
        s, a = state
    panel_out = jnp.concatenate(own, axis=2)[None]

    partial = run_pairs(top_kernel, positions, slices, None, top_pairs.shape[1], 4, "top_products")
    summed = lax.psum_scatter(partial, "leaf", scatter_dimension=0, tiled=True).astype(jnp.float32)
    updated = run_pairs(
        local_kernel, pairs, slices, local_targets[0], local_targets.shape[1], 8, "local_updates"
    )
    top_out = (top_targets[0].astype(jnp.float32) - summed).astype(jnp.bfloat16)[None]
    return (panel_out, updated[None], top_out)


def solution(mesh):
    in_specs = (
        P("leaf", None, None),
        P("leaf", "blk", None, None),
        P("leaf", "blk", None, None),
        P("leaf", "blk", None),
        P("blk", "leaf", None, None),
        P("blk", None, None),
        P("leaf", None),
    )
    out_specs = (
        P("leaf", "blk", None, None),
        P("leaf", "blk", None, None),
        P("blk", "leaf", None, None),
    )
    return jax.shard_map(
        on_device, mesh=mesh, in_specs=in_specs, out_specs=out_specs, check_vma=False
    )
```

```python
import functools

import jax
import jax.numpy as jnp
from jax import lax
from jax.experimental import pallas as pl
from jax.experimental.pallas import tpu as pltpu
from jax.sharding import PartitionSpec as P

NB = 128
MESH = pl.DeviceIdType.MESH
HI = lax.Precision.HIGHEST
VMEM_LIMIT = 56 * 1024 * 1024


def mm(a, b, contract, precision=HI):
    return lax.dot_general(
        a, b, ((contract[:1], contract[1:]), ((), ())),
        precision=precision, preferred_element_type=jnp.float32,
    )


def eliminate(block, inv_ref, midway):
    d = block
    row = lax.broadcasted_iota(jnp.int32, (NB, NB), 0)
    col = lax.broadcasted_iota(jnp.int32, (NB, NB), 1)
    e = jnp.where(row == col, 1.0, 0.0).astype(jnp.float32)
    top = 0
    for j in range(NB):
        if j - top == 16:
            d, e, top = d[16:], e[16:], j
        if j == NB // 2:
            midway()
        r = j - top
        drow = d[r:r + 1, :]
        erow = e[r:r + 1, :]
        pivot = jnp.broadcast_to(drow[:, j:j + 1], (1, NB))
        inv_ref[j:j + 1, :] = erow * lax.rsqrt(pivot)
        inverse = 1.0 / pivot
        factor = jnp.broadcast_to(d[:, j:j + 1], d.shape)
        d = d - factor * (drow * inverse)
        e = e - factor * (erow * inverse)


def factor_kernel(
    stages, s_in, a_in, x_all, panel_out, s_ref, a_ref, inv_ref, x_ref,
    own_sem, net_send, down_send, net_recv, part_send, part_recv,
):
    leaf, blk = lax.axis_index("leaf"), lax.axis_index("blk")
    z, core = lax.div(blk, 2), lax.rem(blk, 2)
    partner = 2 * z + 1 - core
    slices, count, width = x_ref.shape[:3]
    last = stages - 1

    barrier = pltpu.get_barrier_semaphore()

    def signal(target):
        pl.semaphore_signal(barrier, inc=1, device_id=(leaf, target), device_id_type=MESH)

    signal(partner)

    @pl.when(z < last)
    def _():
        signal(blk + 2)

    @pl.when(z > 0)
    def _():
        signal(blk - 2)

    def chunk(q, origin, lane):
        return x_all.at[q, pl.ds((2 * origin + lane) * count, count)]

    def remote(src, q, origin, lane, send, recv, target):
        return pltpu.make_async_remote_copy(
            src_ref=src, dst_ref=chunk(q, origin, lane), send_sem=send, recv_sem=recv,
            device_id=(leaf, target), device_id_type=MESH,
        )

    def net(src, q, origin, target):
        return remote(src, q, origin, core, net_send.at[q, origin], net_recv.at[q, origin], target)

    def down_own(q):
        return remote(x_ref.at[q], q, z, core, down_send.at[q], net_recv.at[q, z], blk - 2)

    def across(src, q, origin):
        return remote(src, q, origin, core, part_send.at[q, origin], part_recv.at[q, origin], partner)

    def local(q):
        return pltpu.make_async_copy(x_ref.at[q], chunk(q, z, core), own_sem.at[q])

    def send_own(q):
        @pl.when(z < last)
        def _():
            net(x_ref.at[q], q, z, blk + 2).start()

        @pl.when(z > 0)
        def _():
            down_own(q).start()

        across(x_ref.at[q], q, z).start()
        local(q).start()

    def forward(q, hop):
        above, below = z - hop, z + hop

        @pl.when(above >= 0)
        def _():
            held = chunk(q, above, core)
            net(held, q, above, blk).wait_recv()

            @pl.when(z < last)
            def _():
                net(held, q, above, blk + 2).start()

            across(held, q, above).start()

        @pl.when(below <= last)
        def _():
            held = chunk(q, below, core)
            net(held, q, below, blk).wait_recv()

            @pl.when(z > 0)
            def _():
                net(held, q, below, blk - 2).start()

            across(held, q, below).start()

    def forwards(tick):
        for q in range(slices):
            hop = tick - 2 * q
            if 1 <= hop <= last:
                forward(q, hop)

    for q in range(slices):
        s_now, a_now = (s_in, a_in) if q == 0 else (s_ref, a_ref)
        at = q * NB
        eliminate(s_now[at:at + NB, at:at + NB], inv_ref, lambda: forwards(2 * q - 1))
        inverse = inv_ref[...]
        x = mm(a_now[:, at:at + NB], inverse, (1, 1))
        rounded = x.astype(x_ref.dtype)
        x_ref[q] = rounded.reshape(count, width, NB)
        panel_out[:, at:at + NB] = rounded
        if q == 0:
            pl.semaphore_wait(barrier, 1 + jnp.minimum(z, 1) + jnp.minimum(last - z, 1))

        send_own(q)
        forwards(2 * q)
        if q < slices - 1:
            upper = mm(inverse, s_now[at:at + NB, at + NB:], (1, 0))
            s_ref[at + NB:, at + NB:] = s_now[at + NB:, at + NB:] - mm(upper, upper, (0, 0))
            a_ref[:, at + NB:] = a_now[:, at + NB:] - mm(x, upper, (1, 0))

    for tick in range(2 * slices - 1, 2 * slices - 1 + last):
        forwards(tick)

    for q in range(slices):
        local(q).wait()

        @pl.when(z > 0)
        def _():
            down_own(q).wait_send()

        for origin in range(stages):
            held = chunk(q, origin, core)
            across(held, q, origin).wait_send()
            remote(
                held, q, origin, 1 - core,
                part_send.at[q, origin], part_recv.at[q, origin], partner,
            ).wait_recv()

            @pl.when(((origin <= z) & (z < last)) | ((origin > z) & (z > 0)))
            def _():
                net(held, q, origin, blk).wait_send()


def run_factor(s, a, count, parts):
    order, rows = s.shape[0], a.shape[0]
    slices, stages, width = order // NB, parts // 2, rows // count
    vmem = pl.BlockSpec(memory_space=pltpu.VMEM)
    dma = pltpu.SemaphoreType.DMA
    return pl.pallas_call(
        functools.partial(factor_kernel, stages),
        out_shape=[
            jax.ShapeDtypeStruct((slices, parts * count, width, NB), jnp.bfloat16),
            jax.ShapeDtypeStruct((rows, order), jnp.bfloat16),
        ],
        in_specs=[vmem, vmem],
        out_specs=[pl.BlockSpec(memory_space=pl.ANY), vmem],
        scratch_shapes=[
            pltpu.VMEM((order, order), jnp.float32),
            pltpu.VMEM((rows, order), jnp.float32),
            pltpu.VMEM((NB, NB), jnp.float32),
            pltpu.VMEM((slices, count, width, NB), jnp.bfloat16),
            dma((slices,)),
            dma((slices, stages)),
            dma((slices,)),
            dma((slices, stages)),
            dma((slices, stages)),
            dma((slices, stages)),
        ],
        compiler_params=pltpu.CompilerParams(
            vmem_limit_bytes=VMEM_LIMIT, collective_id=0, has_side_effects=True
        ),
        cost_estimate=pl.CostEstimate(flops=80_000_000_000, bytes_accessed=16_000_000, transcendentals=0),
        name="factor_and_gather",
    )(s, a)


def product(rows, p, q):
    slices = range(rows.shape[0])
    left = jnp.concatenate([rows[k, jnp.maximum(p, 0)] for k in slices], axis=1)
    right = jnp.concatenate([rows[k, jnp.maximum(q, 0)] for k in slices], axis=1)
    live = (p >= 0) & (q >= 0)
    return jnp.where(live, mm(left, right, (1, 1), None), 0.0)


def top_kernel(pairs, rows, *outs):
    per_out = outs[0].shape[0]
    for k in range(len(outs)):
        for s in range(per_out):
            at = k * per_out + s
            outs[k][s] = product(rows, pairs[0, at], pairs[1, at]).astype(outs[k].dtype)


def run_top(pairs, rows, shares, width):
    per_out = pairs.shape[1] // shares
    vmem = pl.BlockSpec(memory_space=pltpu.VMEM)
    shape = jax.ShapeDtypeStruct((per_out, width, width), jnp.bfloat16)
    return pl.pallas_call(
        top_kernel,
        in_specs=[pl.BlockSpec(memory_space=pltpu.SMEM), vmem],
        out_specs=[vmem] * shares,
        out_shape=[shape] * shares,
        compiler_params=pltpu.CompilerParams(vmem_limit_bytes=VMEM_LIMIT),
        cost_estimate=pl.CostEstimate(flops=1_000_000_000, bytes_accessed=10_000_000, transcendentals=0),
        name="top_products",
    )(pairs, rows)


def local_kernel(per_step, pairs, rows, target, out):
    base = pl.program_id(0) * per_step
    for s in range(per_step):
        fresh = target[s].astype(jnp.float32) - product(rows, pairs[0, base + s], pairs[1, base + s])
        out[s] = fresh.astype(out.dtype)


def run_local(pairs, rows, targets, per_step):
    count, width = targets.shape[:2]
    depth = rows.shape[0] * rows.shape[3]
    whole = pl.BlockSpec(rows.shape, lambda i, pairs: (0, 0, 0, 0), pipeline_mode=pl.Buffered(1))
    block = pl.BlockSpec((per_step, width, width), lambda i, pairs: (i, 0, 0))
    return pl.pallas_call(
        functools.partial(local_kernel, per_step),
        grid_spec=pltpu.PrefetchScalarGridSpec(
            num_scalar_prefetch=1,
            grid=(count // per_step,),
            in_specs=[whole, block],
            out_specs=block,
        ),
        out_shape=jax.ShapeDtypeStruct((count, width, width), jnp.bfloat16),
        compiler_params=pltpu.CompilerParams(vmem_limit_bytes=VMEM_LIMIT),
        cost_estimate=pl.CostEstimate(
            flops=2 * count * width * width * depth,
            bytes_accessed=4 * count * width * width,
            transcendentals=0,
        ),
        name="local_updates",
    )(pairs, rows, targets)


def on_device(leaves, parts, diag_blocks, panel, local_targets, local_pairs, top_targets, top_pairs, top_pattern):
    s = diag_blocks[0]
    count, width, columns = panel.shape[1:]
    a = panel[0].reshape(count * width, columns)
    pattern = top_pattern[0]
    ancestors = jnp.arange(pattern.shape[0], dtype=jnp.int32)

    def lookup(ids):
        return jnp.sum(jnp.where(ids[:, None] == ancestors[None, :], pattern[None, :], 0), axis=1)

    owners = lax.axis_index("leaf") ^ jnp.arange(leaves, dtype=jnp.int32)
    pairs_by_share = top_pairs[0].reshape(leaves, -1, 2)[owners].reshape(-1, 2)
    positions = jnp.stack([lookup(pairs_by_share[:, 0]), lookup(pairs_by_share[:, 1])])

    rows, panel_out = run_factor(s, a, count, parts)
    shares = run_top(positions, rows, leaves, width)
    arrived = [
        lax.ppermute(shares[m], "leaf", [(i, i ^ m) for i in range(leaves)])
        for m in range(1, leaves)
    ]
    updated = run_local(local_pairs[0].T, rows, local_targets[0], 8)
    summed = shares[0].astype(jnp.float32)
    for term in arrived:
        summed = summed + term.astype(jnp.float32)
    top_out = (top_targets[0].astype(jnp.float32) - summed).astype(jnp.bfloat16)[None]
    return (panel_out.reshape(panel.shape), updated[None], top_out)


def solution(mesh):
    in_specs = (
        P("leaf", None, None),
        P("leaf", "blk", None, None),
        P("leaf", "blk", None, None),
        P("leaf", "blk", None),
        P("blk", "leaf", None, None),
        P("blk", None, None),
        P("leaf", None),
    )
    out_specs = (
        P("leaf", "blk", None, None),
        P("leaf", "blk", None, None),
        P("blk", "leaf", None, None),
    )
    return jax.shard_map(
        functools.partial(on_device, mesh.shape["leaf"], mesh.shape["blk"]),
        mesh=mesh, in_specs=in_specs, out_specs=out_specs, check_vma=False
    )
```

```python
import functools

import jax
import jax.numpy as jnp
from jax import lax
from jax.experimental import pallas as pl
from jax.experimental.pallas import tpu as pltpu
from jax.sharding import PartitionSpec as P

NB = 128
AT_ONCE = 4
MESH = pl.DeviceIdType.MESH
HI = lax.Precision.HIGHEST
VMEM_LIMIT = 56 * 1024 * 1024


def mm(a, b, contract, precision=HI):
    return lax.dot_general(
        a, b, ((contract[:1], contract[1:]), ((), ())),
        precision=precision, preferred_element_type=jnp.float32,
    )


def eliminate(block, inv_ref, midway):
    d = block
    row = lax.broadcasted_iota(jnp.int32, (NB, NB), 0)
    col = lax.broadcasted_iota(jnp.int32, (NB, NB), 1)
    e = jnp.where(row == col, 1.0, 0.0).astype(jnp.float32)
    top = 0
    for j in range(0, NB, AT_ONCE):
        if j - top == 16:
            d, e, top = d[16:], e[16:], j
        if j == NB // 2:
            midway()
        r = j - top
        drow = [d[r + i:r + i + 1, :] for i in range(AT_ONCE)]
        erow = [e[r + i:r + i + 1, :] for i in range(AT_ONCE)]
        factor = [jnp.broadcast_to(d[:, j + i:j + i + 1], d.shape) for i in range(AT_ONCE)]
        for i in range(AT_ONCE):
            pivot = factor[i][r + i:r + i + 1, :]
            inv_ref[j + i:j + i + 1, :] = erow[i] * lax.rsqrt(pivot)
            inverse = 1.0 / pivot
            drow[i] = drow[i] * inverse
            erow[i] = erow[i] * inverse
            for k in range(i + 1, AT_ONCE):
                below = factor[i][r + k:r + k + 1, :]
                drow[k] = drow[k] - below * drow[i]
                erow[k] = erow[k] - below * erow[i]
                factor[k] = factor[k] - factor[i] * (factor[k][r + i:r + i + 1, :] * inverse)
        for i in range(AT_ONCE):
            d = d - factor[i] * drow[i]
            e = e - factor[i] * erow[i]


def factor_kernel(
    stages, s_in, a_in, x_all, s_ref, a_ref, inv_ref, x_ref,
    own_sem, net_send, down_send, net_recv, part_send, part_recv,
):
    leaf, blk = lax.axis_index("leaf"), lax.axis_index("blk")
    z, core = lax.div(blk, 2), lax.rem(blk, 2)
    partner = 2 * z + 1 - core
    slices, count, width = x_ref.shape[:3]
    last = stages - 1

    barrier = pltpu.get_barrier_semaphore()

    def signal(target):
        pl.semaphore_signal(barrier, inc=1, device_id=(leaf, target), device_id_type=MESH)

    signal(partner)

    @pl.when(z < last)
    def _():
        signal(blk + 2)

    @pl.when(z > 0)
    def _():
        signal(blk - 2)

    def chunk(q, origin, lane):
        return x_all.at[q, pl.ds((2 * origin + lane) * count, count)]

    def remote(src, q, origin, lane, send, recv, target):
        return pltpu.make_async_remote_copy(
            src_ref=src, dst_ref=chunk(q, origin, lane), send_sem=send, recv_sem=recv,
            device_id=(leaf, target), device_id_type=MESH,
        )

    def net(src, q, origin, target):
        return remote(src, q, origin, core, net_send.at[q, origin], net_recv.at[q, origin], target)

    def down_own(q):
        return remote(x_ref.at[q], q, z, core, down_send.at[q], net_recv.at[q, z], blk - 2)

    def across(src, q, origin):
        return remote(src, q, origin, core, part_send.at[q, origin], part_recv.at[q, origin], partner)

    def local(q):
        return pltpu.make_async_copy(x_ref.at[q], chunk(q, z, core), own_sem.at[q])

    def send_own(q):
        @pl.when(z < last)
        def _():
            net(x_ref.at[q], q, z, blk + 2).start()

        @pl.when(z > 0)
        def _():
            down_own(q).start()

        across(x_ref.at[q], q, z).start()
        local(q).start()

    def forward(q, hop):
        above, below = z - hop, z + hop

        @pl.when(above >= 0)
        def _():
            held = chunk(q, above, core)
            net(held, q, above, blk).wait_recv()

            @pl.when(z < last)
            def _():
                net(held, q, above, blk + 2).start()

            across(held, q, above).start()

        @pl.when(below <= last)
        def _():
            held = chunk(q, below, core)
            net(held, q, below, blk).wait_recv()

            @pl.when(z > 0)
            def _():
                net(held, q, below, blk - 2).start()

            across(held, q, below).start()

    def forwards(tick):
        for q in range(slices):
            hop = tick - 2 * q
            if 1 <= hop <= last:
                forward(q, hop)

    for q in range(slices):
        s_now, a_now = (s_in, a_in) if q == 0 else (s_ref, a_ref)
        at = q * NB
        eliminate(s_now[at:at + NB, at:at + NB], inv_ref, lambda: forwards(2 * q - 1))
        inverse = inv_ref[...]
        x = mm(a_now[:, at:at + NB], inverse, (1, 1))
        x_ref[q] = x.astype(x_ref.dtype).reshape(count, width, NB)
        if q == 0:
            pl.semaphore_wait(barrier, 1 + jnp.minimum(z, 1) + jnp.minimum(last - z, 1))

        send_own(q)
        forwards(2 * q)
        if q < slices - 1:
            upper = mm(inverse, s_now[at:at + NB, at + NB:], (1, 0))
            s_ref[at + NB:, at + NB:] = s_now[at + NB:, at + NB:] - mm(upper, upper, (0, 0))
            a_ref[:, at + NB:] = a_now[:, at + NB:] - mm(x, upper, (1, 0))

    for tick in range(2 * slices - 1, 2 * slices - 1 + last):
        forwards(tick)

    for q in range(slices):
        local(q).wait()

        @pl.when(z > 0)
        def _():
            down_own(q).wait_send()

        for origin in range(stages):
            held = chunk(q, origin, core)
            across(held, q, origin).wait_send()
            remote(
                held, q, origin, 1 - core,
                part_send.at[q, origin], part_recv.at[q, origin], partner,
            ).wait_recv()

            @pl.when(((origin <= z) & (z < last)) | ((origin > z) & (z > 0)))
            def _():
                net(held, q, origin, blk).wait_send()


def run_factor(s, a, count, parts):
    order, rows = s.shape[0], a.shape[0]
    slices, stages, width = order // NB, parts // 2, rows // count
    vmem = pl.BlockSpec(memory_space=pltpu.VMEM)
    dma = pltpu.SemaphoreType.DMA
    return pl.pallas_call(
        functools.partial(factor_kernel, stages),
        out_shape=jax.ShapeDtypeStruct((slices, parts * count, width, NB), jnp.bfloat16),
        in_specs=[vmem, vmem],
        out_specs=pl.BlockSpec(memory_space=pl.ANY),
        scratch_shapes=[
            pltpu.VMEM((order, order), jnp.float32),
            pltpu.VMEM((rows, order), jnp.float32),
            pltpu.VMEM((NB, NB), jnp.float32),
            pltpu.VMEM((slices, count, width, NB), jnp.bfloat16),
            dma((slices,)),
            dma((slices, stages)),
            dma((slices,)),
            dma((slices, stages)),
            dma((slices, stages)),
            dma((slices, stages)),
        ],
        compiler_params=pltpu.CompilerParams(
            vmem_limit_bytes=VMEM_LIMIT, collective_id=0, has_side_effects=True
        ),
        cost_estimate=pl.CostEstimate(flops=80_000_000_000, bytes_accessed=16_000_000, transcendentals=0),
        name="factor_and_gather",
    )(s, a)


def product(rows, p, q):
    slices = range(rows.shape[0])
    left = jnp.concatenate([rows[k, jnp.maximum(p, 0)] for k in slices], axis=1)
    right = jnp.concatenate([rows[k, jnp.maximum(q, 0)] for k in slices], axis=1)
    live = (p >= 0) & (q >= 0)
    return jnp.where(live, mm(left, right, (1, 1), None), 0.0)


def top_kernel(pairs, pattern, rows, *outs):
    per_out = outs[0].shape[0]
    leaf = lax.axis_index("leaf")
    for k in range(len(outs)):
        base = (leaf ^ k) * per_out
        for s in range(per_out):
            p, q = pattern[0, pairs[0, base + s]], pattern[0, pairs[1, base + s]]
            outs[k][s] = product(rows, p, q).astype(outs[k].dtype)


def run_top(pairs, pattern, rows, shares, width):
    per_out = pairs.shape[1] // shares
    vmem = pl.BlockSpec(memory_space=pltpu.VMEM)
    shape = jax.ShapeDtypeStruct((per_out, width, width), jnp.bfloat16)
    return pl.pallas_call(
        top_kernel,
        in_specs=[pl.BlockSpec(memory_space=pltpu.SMEM)] * 2 + [vmem],
        out_specs=[vmem] * shares,
        out_shape=[shape] * shares,
        compiler_params=pltpu.CompilerParams(vmem_limit_bytes=VMEM_LIMIT),
        cost_estimate=pl.CostEstimate(flops=1_000_000_000, bytes_accessed=10_000_000, transcendentals=0),
        name="top_products",
    )(pairs, pattern, rows)


def local_kernel(per_step, pairs, rows, target, out, own):
    base = pl.program_id(0) * per_step

    @pl.when(base == 0)
    def _():
        first = lax.axis_index("blk") * own.shape[0]
        for i in range(own.shape[0]):
            for k in range(rows.shape[0]):
                own[i, :, k * NB:(k + 1) * NB] = rows[k, first + i]

    for s in range(per_step):
        fresh = target[s].astype(jnp.float32) - product(rows, pairs[0, base + s], pairs[1, base + s])
        out[s] = fresh.astype(out.dtype)


def run_local(pairs, rows, targets, own_count, per_step):
    count, width = targets.shape[:2]
    depth = rows.shape[0] * rows.shape[3]
    whole = pl.BlockSpec(rows.shape, lambda i, pairs: (0, 0, 0, 0), pipeline_mode=pl.Buffered(1))
    block = pl.BlockSpec((per_step, width, width), lambda i, pairs: (i, 0, 0))
    return pl.pallas_call(
        functools.partial(local_kernel, per_step),
        grid_spec=pltpu.PrefetchScalarGridSpec(
            num_scalar_prefetch=1,
            grid=(count // per_step,),
            in_specs=[whole, block],
            out_specs=[block, pl.BlockSpec((own_count, width, depth), lambda i, pairs: (0, 0, 0))],
        ),
        out_shape=[
            jax.ShapeDtypeStruct((count, width, width), jnp.bfloat16),
            jax.ShapeDtypeStruct((own_count, width, depth), jnp.bfloat16),
        ],
        compiler_params=pltpu.CompilerParams(vmem_limit_bytes=VMEM_LIMIT),
        cost_estimate=pl.CostEstimate(
            flops=2 * count * width * width * depth,
            bytes_accessed=4 * count * width * width,
            transcendentals=0,
        ),
        name="local_updates",
    )(pairs, rows, targets)


def on_device(leaves, parts, diag_blocks, panel, local_targets, local_pairs, top_targets, top_pairs, top_pattern):
    s = diag_blocks[0]
    count, width, columns = panel.shape[1:]
    a = panel[0].reshape(count * width, columns)
    rows = run_factor(s, a, count, parts)
    shares = run_top(top_pairs[0].T, top_pattern, rows, leaves, width)
    arrived = [
        lax.ppermute(shares[m], "leaf", [(i, i ^ m) for i in range(leaves)])
        for m in range(1, leaves)
    ]
    updated, panel_out = run_local(local_pairs[0].T, rows, local_targets[0], count, 8)
    summed = shares[0].astype(jnp.float32)
    for term in arrived:
        summed = summed + term.astype(jnp.float32)
    top_out = (top_targets[0].astype(jnp.float32) - summed).astype(jnp.bfloat16)[None]
    return (panel_out[None], updated[None], top_out)


def solution(mesh):
    in_specs = (
        P("leaf", None, None),
        P("leaf", "blk", None, None),
        P("leaf", "blk", None, None),
        P("leaf", "blk", None),
        P("blk", "leaf", None, None),
        P("blk", None, None),
        P("leaf", None),
    )
    out_specs = (
        P("leaf", "blk", None, None),
        P("leaf", "blk", None, None),
        P("blk", "leaf", None, None),
    )
    return jax.shard_map(
        functools.partial(on_device, mesh.shape["leaf"], mesh.shape["blk"]),
        mesh=mesh, in_specs=in_specs, out_specs=out_specs, check_vma=False
    )
```
